32 devices in a mesh: row: 4 (over z), col: 8 (over y, x, core).
Axes of the slice: x: 2, y: 2, z: 4, core: 2. Of those that a mesh axis runs over, the one named last changes fastest.
Arguments:
- pretrained_weight: bfloat16 [4096, 53248], P('row', 'col'), may hold values from -45 to 45, as said below
- up_factors: bfloat16 [4096, 2048], P('row', 'col'), may hold values from -0.125 to 0.125
- down_factors: bfloat16 [2048, 53248], P('row', 'col'), may hold values from -6 to 6
- adapter_weights: float32 [32], replicated, may hold values from 0.2 to 1.5
Outputs:
- quantized: bfloat16 [4096, 53248], P(None, ('col', 'row'))
- block_scale: float32 [32, 416], P('row', 'col')
The draws below stay inside these ranges and needn't reach their ends.
Inputs may be any that keep to these rules, and one draw needn't show every extreme that they name: `pretrained_weight`: entries of varied scale from row to row and column to column.
All inputs are finite; a program needn't handle non-finite values. Where the reference program divides by a largest or mean magnitude, that divisor is 1e-20 or more.
Results may differ from the reference program's by a relative error of at most 0.0028.
Values may be sent and summed in bfloat16 or wider, within the bound.
A program may use at most 192 MiB of HBM per device.

```python
import math
import jax
import jax.numpy as jnp
from jax import lax

HIDDEN_UNITS = 53248
ADAPTERS = 32
RANK = 64
QB = 128
TOTAL_RANK = 2048
MATRIX_ROWS = 4096


def draw_pretrained_weight(key, part):
    first, second, third = jax.random.split(jax.random.fold_in(key, 17), 3)
    row_scale = jnp.exp(jax.random.uniform(first, (MATRIX_ROWS, 1), jnp.float32, math.log(0.3), math.log(3.0)))
    col_scale = jnp.exp(jax.random.uniform(second, (1, HIDDEN_UNITS), jnp.float32, math.log(0.3), math.log(3.0)))
    noise = jnp.clip(jax.random.normal(third, (MATRIX_ROWS, HIDDEN_UNITS), jnp.float32), -5.0, 5.0)
    return (noise * row_scale * col_scale).astype(jnp.bfloat16)


def block_scale(stream_key, dims, shards, smallest, top_value):
    loudness, own = 1.0, jax.random.fold_in(stream_key, 6)
    for axis_at, parts in shards:
        draws = jnp.exp(jax.random.uniform(jax.random.fold_in(own, axis_at), (parts,), jnp.float32, smallest / len(shards), top_value / len(shards)))
        loudness = loudness * jnp.repeat(draws, dims[axis_at] // parts).reshape([-1 if axis == axis_at else 1 for axis in range(len(dims))])
    return loudness


def centred(stream_key, shape, scale, bound, shards=(), kind=jnp.bfloat16):
    gain = block_scale(stream_key, shape, shards, -0.22, 0.18) if shards else 1.0
    drawn = jax.random.normal(stream_key, shape, jnp.float32) * scale * gain
    return jnp.minimum(jnp.maximum(drawn, -bound), bound).astype(kind)


def setup_inputs(seed: int = 0) -> dict:
    key_of = jax.random.split(jax.random.key(seed), 5)
    pretrained_weight = draw_pretrained_weight(jax.random.fold_in(key_of[4], 71), 0)
    up_factors = centred(key_of[1], (MATRIX_ROWS, TOTAL_RANK), TOTAL_RANK ** -0.5, 0.125, ((0, 4), (1, 8)))
    down_factors = centred(key_of[2], (TOTAL_RANK, HIDDEN_UNITS), 1.0, 6.0, ((0, 4), (1, 8)))
    adapter_weights = jnp.clip(jnp.exp(jax.random.uniform(key_of[3], (ADAPTERS,), jnp.float32, math.log(0.2), math.log(1.5))), 0.2, 1.5)
    return dict(pretrained_weight=pretrained_weight, up_factors=up_factors, down_factors=down_factors, adapter_weights=adapter_weights)


def reference(pretrained_weight, up_factors, down_factors, adapter_weights):
    broadcast_scales = jnp.repeat(adapter_weights, RANK)
    weighted_up_factors = (up_factors.astype(jnp.float32) * broadcast_scales[None, :]).astype(jnp.bfloat16)
    blocks = MATRIX_ROWS // QB

    def one_block(index):
        start = (index * QB).astype(jnp.int32)
        base_row_slab = lax.dynamic_slice_in_dim(pretrained_weight, start, QB, 0)
        factor_row_slab = lax.dynamic_slice_in_dim(weighted_up_factors, start, QB, 0)
        merged_weight = base_row_slab.astype(jnp.float32) + jnp.dot(factor_row_slab, down_factors, preferred_element_type=jnp.float32)
        tiles = merged_weight.reshape(QB, HIDDEN_UNITS // QB, QB)
        largest = jnp.max(jnp.abs(tiles), axis=(0, 2)) + 1e-6
        values = (tiles / largest[None, :, None]).astype(jnp.bfloat16).reshape(QB, HIDDEN_UNITS)
        return values, largest

    values, largest = lax.map(one_block, jnp.arange(blocks, dtype=jnp.int32))
    return values.reshape(MATRIX_ROWS, HIDDEN_UNITS), largest
```

```python
import functools

import jax
import jax.numpy as jnp
from jax import lax
from jax.experimental import pallas as pl
from jax.experimental.pallas import tpu as pltpu
from jax.sharding import PartitionSpec as P

RANK = 64
QB = 128
CHUNK = 256


def weighted_factors(up_factors, adapter_weights):
    local_rank_slab = up_factors.shape[1]
    broadcast_scales = jnp.repeat(adapter_weights, RANK)
    offset = lax.axis_index("col") * local_rank_slab
    local_scale = lax.dynamic_slice_in_dim(broadcast_scales, offset, local_rank_slab, 0)
    return (up_factors.astype(jnp.float32) * local_scale[None, :]).astype(jnp.bfloat16)


def scale_tiles(merged_weight):
    row_count, col_count = merged_weight.shape
    tiles = merged_weight.reshape(row_count // QB, QB, col_count // QB, QB)
    largest = jnp.max(jnp.abs(tiles), axis=(1, 3)) + 1e-06
    values = (tiles / largest[:, None, :, None]).astype(jnp.bfloat16).reshape(row_count, col_count)
    return (values, largest)


def panel_shards(pretrained_weight, up_factors, down_factors, adapter_weights):
    weighted_update = weighted_factors(up_factors, adapter_weights)
    b_panel = lax.all_gather(weighted_update, "col", axis=1, tiled=True)
    merged_weight = pretrained_weight.astype(jnp.float32) + jnp.dot(
        b_panel,
        lax.all_gather(down_factors, "row", axis=0, tiled=True),
        preferred_element_type=jnp.float32,
    )
    values, largest = scale_tiles(merged_weight)
    serving = lax.all_to_all(values, "row", split_axis=1, concat_axis=0, tiled=True)
    return (serving, largest)


def merge_kernel(
    nr, nc, b_in, a_in, w_in, out, scales_out,
    a_full, b_full, w_full, o_buf, s_own, s_all,
    a_send, a_recv, b_send, b_recv, w_send, w_recv, s_send, s_recv, o_sem, local_sem,
):
    rows, width = w_in.shape
    cols = width // nr
    depth = a_in.shape[0]
    planes = nc // 2
    chunks = rows // CHUNK
    per_chunk = CHUNK // QB
    blocks = cols // QB
    r = lax.axis_index("row")
    c = lax.axis_index("col")
    chip, core = c // 2, lax.rem(c, 2)
    sibling = chip * 2 + (1 - core)

    def z_peer(i):
        return lax.rem(r + i, nr)

    def plane_peer(i):
        return lax.rem(chip + i, planes) * 2 + core

    barrier = pltpu.get_barrier_semaphore()
    for i in range(1, nr):
        pl.semaphore_signal(barrier, inc=1, device_id={"row": z_peer(i)}, device_id_type=pl.DeviceIdType.MESH)
    for i in range(1, planes):
        pl.semaphore_signal(barrier, inc=1, device_id={"col": plane_peer(i)}, device_id_type=pl.DeviceIdType.MESH)
    pl.semaphore_signal(barrier, inc=1, device_id={"col": sibling}, device_id_type=pl.DeviceIdType.MESH)
    pl.semaphore_wait(barrier, nr - 1 + planes - 1 + 1)

    def columns(j):
        return pl.ds(pl.multiple_of(j * cols, QB), cols)

    def b_z(i, src, slot):
        return pltpu.make_async_remote_copy(
            src_ref=src, dst_ref=b_full.at[slot[1], pl.ds(slot[0] * rows, rows), :],
            send_sem=b_send.at[0, i], recv_sem=b_recv.at[slot[0], slot[1]],
            device_id={"row": z_peer(i)}, device_id_type=pl.DeviceIdType.MESH)

    def b_slot(j, q):
        return b_full.at[q, pl.ds(j * rows, rows), :]

    for i in range(1, nr):
        pltpu.make_async_remote_copy(
            src_ref=b_in, dst_ref=b_slot(r, c), send_sem=b_send.at[0, i], recv_sem=b_recv.at[r, c],
            device_id={"row": z_peer(i)}, device_id_type=pl.DeviceIdType.MESH).start()
    for i in range(1, nr):
        pltpu.make_async_remote_copy(
            src_ref=a_in.at[:, columns(z_peer(i))], dst_ref=a_full.at[pl.ds(r * depth, depth), :],
            send_sem=a_send.at[i], recv_sem=a_recv.at[r],
            device_id={"row": z_peer(i)}, device_id_type=pl.DeviceIdType.MESH).start()
    own_a = pltpu.make_async_copy(a_in.at[:, columns(r)], a_full.at[pl.ds(r * depth, depth), :], local_sem.at[0])
    own_a.start()
    own_b = pltpu.make_async_copy(b_in, b_slot(r, c), local_sem.at[1])
    own_b.start()
    own_w = pltpu.make_async_copy(w_in.at[:, columns(r)], w_full.at[pl.ds(r * rows, rows), :], local_sem.at[2])
    own_w.start()

    def w_copy(i, t):
        source = pl.multiple_of(t * CHUNK, CHUNK)
        return pltpu.make_async_remote_copy(
            src_ref=w_in.at[pl.ds(source, CHUNK), columns(z_peer(i))],
            dst_ref=w_full.at[pl.ds(pl.multiple_of(r * rows + t * CHUNK, CHUNK), CHUNK), :],
            send_sem=w_send.at[i, t], recv_sem=w_recv.at[r, t],
            device_id={"row": z_peer(i)}, device_id_type=pl.DeviceIdType.MESH)

    @pl.loop(0, chunks)
    def _(t):
        for i in range(1, nr):
            w_copy(i, t).start()

    def b_wait(j, q):
        slot = b_slot(j, q)
        pltpu.make_async_copy(slot, slot, b_recv.at[j, q]).wait()

    def b_share(k, j, q, to, src):
        return pltpu.make_async_remote_copy(
            src_ref=src, dst_ref=b_slot(j, q), send_sem=b_send.at[1 + k[0], k[1]], recv_sem=b_recv.at[j, q],
            device_id={"col": to}, device_id_type=pl.DeviceIdType.MESH)

    own_b.wait()

    def spread(m, j):
        for i in range(1, planes):
            b_share((m, i), j, c, plane_peer(i), b_slot(j, c)).start()
        b_share((m, planes), j, c, sibling, b_slot(j, c)).start()

    spread(0, r)
    for m in range(1, nr):
        j = z_peer(m)
        b_wait(j, c)
        spread(m, j)
    for m in range(nr):
        j = z_peer(m)
        for i in range(1, planes):
            q = plane_peer(i)
            b_wait(j, q)
            b_share((m, planes + i), j, q, sibling, b_slot(j, q)).start()
    for m in range(nr):
        j = z_peer(m)
        for i in range(planes):
            b_wait(j, lax.rem(chip + i, planes) * 2 + (1 - core))

    own_a.wait()
    for i in range(1, nr):
        part = a_full.at[pl.ds(z_peer(i) * depth, depth), :]
        pltpu.make_async_copy(part, part, a_recv.at[z_peer(i)]).wait()

    def merge_cols(slot, j, t, col, count):
        row = pl.multiple_of(j * rows + t * CHUNK, CHUNK)
        at = pl.ds(row, CHUNK)
        lhs = jnp.concatenate([b_full[q, at, :] for q in range(nc)], axis=1)
        part = pl.ds(pl.multiple_of(col * QB, QB), count * QB)
        merged = w_full[at, part].astype(jnp.float32) + jnp.dot(
            lhs, a_full[:, part], preferred_element_type=jnp.float32)
        for y in range(per_chunk):
            for x in range(count):
                tile = merged[y * QB:(y + 1) * QB, x * QB:(x + 1) * QB]
                largest = jnp.max(jnp.max(jnp.abs(tile), axis=0, keepdims=True), axis=1, keepdims=True) + 1e-06
                o_buf[slot, y * QB:(y + 1) * QB, pl.ds(pl.multiple_of((col + x) * QB, QB), QB)] = (
                    tile / largest).astype(jnp.bfloat16)
                s_own[j, t * per_chunk + y, pl.ds(col + x, 1), :] = jnp.broadcast_to(largest, (1, QB))

    def o_copy(slot, j, t):
        return pltpu.make_async_copy(
            o_buf.at[slot], out.at[pl.ds(pl.multiple_of(j * rows + t * CHUNK, CHUNK), CHUNK), :], o_sem.at[slot])

    def merge_chunk(n, j, t):
        slot = lax.rem(n, 2)

        @pl.when(n >= 2)
        def _():
            o_copy(slot, j, t).wait()

        @pl.loop(0, blocks // 2)
        def _(pair):
            merge_cols(slot, j, t, pair * 2, 2)

        if blocks % 2:
            merge_cols(slot, j, t, blocks - 1, 1)
        o_copy(slot, j, t).start()

    own_w.wait()

    @pl.loop(0, chunks)
    def _(t):
        merge_chunk(t, r, t)

    @pl.loop(0, chunks * (nr - 1))
    def _(n):
        t = n // (nr - 1)
        j = lax.rem(r + 1 + lax.rem(n, nr - 1), nr)
        part = w_full.at[pl.ds(pl.multiple_of(j * rows + t * CHUNK, CHUNK), CHUNK), :]
        pltpu.make_async_copy(part, part, w_recv.at[j, t]).wait()
        merge_chunk(n + chunks, j, t)

    def s_copy(i):
        return pltpu.make_async_remote_copy(
            src_ref=s_own.at[z_peer(i)], dst_ref=s_all.at[r], send_sem=s_send.at[i], recv_sem=s_recv.at[r],
            device_id={"row": z_peer(i)}, device_id_type=pl.DeviceIdType.MESH)

    for i in range(1, nr):
        s_copy(i).start()
    s_all[r] = s_own[r]
    for slot in range(2):
        o_copy(slot, r, slot).wait()
    for i in range(1, nr):
        pltpu.make_async_copy(s_own.at[0], s_all.at[z_peer(i)], s_recv.at[z_peer(i)]).wait()
    to_out = pltpu.make_async_copy(s_all, scales_out, local_sem.at[3])
    to_out.start()

    for i in range(1, nr):
        s_copy(i).wait_send()
        pltpu.make_async_copy(b_in, b_in, b_send.at[0, i]).wait()
        part = a_full.at[pl.ds(r * depth, depth), :]
        pltpu.make_async_copy(part, part, a_send.at[i]).wait()
    for m in range(nr):
        for k in range(1, 2 * planes):
            pltpu.make_async_copy(b_in, b_in, b_send.at[1 + m, k]).wait()

    @pl.loop(0, chunks)
    def _(t):
        for i in range(1, nr):
            w_copy(i, t).wait_send()

    to_out.wait()


def merge(nr, nc, b, a, w):
    rows, width = w.shape
    cols = width // nr
    depth = a.shape[0]
    chunks = rows // CHUNK
    blocks = cols // QB
    dma = pltpu.SemaphoreType.DMA
    return pl.pallas_call(
        functools.partial(merge_kernel, nr, nc),
        out_shape=[
            jax.ShapeDtypeStruct((nr * rows, cols), jnp.bfloat16),
            jax.ShapeDtypeStruct((nr, rows // QB, blocks, QB), jnp.float32),
        ],
        in_specs=[pl.BlockSpec(memory_space=pl.ANY)] * 3,
        out_specs=[pl.BlockSpec(memory_space=pl.ANY)] * 2,
        scratch_shapes=[
            pltpu.VMEM((nr * depth, cols), jnp.bfloat16),
            pltpu.VMEM((nc, nr * rows, b.shape[1]), jnp.bfloat16),
            pltpu.VMEM((nr * rows, cols), jnp.bfloat16),
            pltpu.VMEM((2, CHUNK, cols), jnp.bfloat16),
            pltpu.VMEM((nr, rows // QB, blocks, QB), jnp.float32),
            pltpu.VMEM((nr, rows // QB, blocks, QB), jnp.float32),
            dma((nr,)), dma((nr,)),
            dma((nr + 1, nc)), dma((nr, nc)),
            dma((nr, chunks)), dma((nr, chunks)),
            dma((nr,)), dma((nr,)),
            dma((2,)), dma((4,)),
        ],
        compiler_params=pltpu.CompilerParams(
            collective_id=0, has_side_effects=True, vmem_limit_bytes=60 * 2 ** 20),
        cost_estimate=pl.CostEstimate(
            flops=2 * nr * rows * nr * depth * cols, bytes_accessed=4 * rows * width, transcendentals=0),
    )(b, a, w)


def serving_shards(nr, nc, pretrained_weight, up_factors, down_factors, adapter_weights):
    weighted_update = weighted_factors(up_factors, adapter_weights)
    values, scales = merge(nr, nc, weighted_update, down_factors, pretrained_weight)
    largest = jnp.transpose(scales[:, :, :, 0], (1, 0, 2)).reshape(scales.shape[1], -1)
    return (values, largest)


def solution(mesh):
    nr, nc = mesh.shape["row"], mesh.shape["col"]

    def shards(pretrained_weight, up_factors, down_factors, adapter_weights):
        rows, width = pretrained_weight.shape
        whole_blocks = width % (nr * QB) == 0 and rows % CHUNK == 0 and nc % 2 == 0
        if whole_blocks and up_factors.shape[1] % QB == 0:
            return serving_shards(nr, nc, pretrained_weight, up_factors, down_factors, adapter_weights)
        return panel_shards(pretrained_weight, up_factors, down_factors, adapter_weights)

    return jax.shard_map(
        shards,
        mesh=mesh,
        in_specs=(P("row", "col"), P("row", "col"), P("row", "col"), P()),
        out_specs=(P(None, ("col", "row")), P("row", "col")),
        check_vma=False,
    )
```

```python
import functools

import jax
import jax.numpy as jnp
from jax import lax
from jax.experimental import pallas as pl
from jax.experimental.pallas import tpu as pltpu
from jax.sharding import PartitionSpec as P

RANK = 64
QB = 128
CHUNK = 256


def weighted_factors(up_factors, adapter_weights):
    local_rank_slab = up_factors.shape[1]
    broadcast_scales = jnp.repeat(adapter_weights, RANK)
    offset = lax.axis_index("col") * local_rank_slab
    local_scale = lax.dynamic_slice_in_dim(broadcast_scales, offset, local_rank_slab, 0)
    return (up_factors.astype(jnp.float32) * local_scale[None, :]).astype(jnp.bfloat16)


def scale_tiles(merged_weight):
    row_count, col_count = merged_weight.shape
    tiles = merged_weight.reshape(row_count // QB, QB, col_count // QB, QB)
    largest = jnp.max(jnp.abs(tiles), axis=(1, 3)) + 1e-06
    values = (tiles / largest[:, None, :, None]).astype(jnp.bfloat16).reshape(row_count, col_count)
    return (values, largest)


def panel_shards(pretrained_weight, up_factors, down_factors, adapter_weights):
    weighted_update = weighted_factors(up_factors, adapter_weights)
    b_panel = lax.all_gather(weighted_update, "col", axis=1, tiled=True)
    merged_weight = pretrained_weight.astype(jnp.float32) + jnp.dot(
        b_panel,
        lax.all_gather(down_factors, "row", axis=0, tiled=True),
        preferred_element_type=jnp.float32,
    )
    values, largest = scale_tiles(merged_weight)
    serving = lax.all_to_all(values, "row", split_axis=1, concat_axis=0, tiled=True)
    return (serving, largest)


def merge_kernel(
    nr, nc, s_in, b_in, a_in, w_in, w_full, scales_out,
    a_full, b_raw, b_full, s_own, s_all,
    a_send, a_recv, b_send, b_recv, line_send, w_send, w_recv, s_send, s_recv, local_sem,
):
    rows, width = w_in.shape
    cols = width // nr
    depth = a_in.shape[0]
    planes = nc // 2
    chunks = rows // CHUNK
    per_chunk = CHUNK // QB
    blocks = cols // QB
    r = lax.axis_index("row")
    c = lax.axis_index("col")
    chip, core = c // 2, lax.rem(c, 2)
    sibling = chip * 2 + (1 - core)

    def z_peer(i):
        return lax.rem(r + i, nr)

    def plane_peer(i):
        return lax.rem(chip + i, planes) * 2 + core

    barrier = pltpu.get_barrier_semaphore()
    for i in range(1, nr):
        pl.semaphore_signal(barrier, inc=1, device_id={"row": z_peer(i)}, device_id_type=pl.DeviceIdType.MESH)
    for i in range(1, planes):
        pl.semaphore_signal(barrier, inc=1, device_id={"col": plane_peer(i)}, device_id_type=pl.DeviceIdType.MESH)
    pl.semaphore_signal(barrier, inc=1, device_id={"col": sibling}, device_id_type=pl.DeviceIdType.MESH)
    pl.semaphore_wait(barrier, nr - 1 + planes - 1 + 1)

    def columns(j):
        return pl.ds(pl.multiple_of(j * cols, QB), cols)

    def b_slot(j, q):
        return b_full.at[q, pl.ds(j * rows, rows), :]

    half = nr // 2
    own_half = r // half * half
    gate = jnp.where(own_half == 0, half, half - 1)
    inner = jnp.where(own_half == 0, half - 1, half)

    def mate(m):
        return own_half + lax.rem(r - own_half + m, half)

    def b_plane(j, to):
        return pltpu.make_async_remote_copy(
            src_ref=b_slot(j, c), dst_ref=b_slot(j, c), send_sem=line_send.at[j, to], recv_sem=b_recv.at[j, c],
            device_id={"row": to}, device_id_type=pl.DeviceIdType.MESH)

    load = pltpu.make_async_copy(b_in, b_raw, local_sem.at[1])
    load.start()
    own_a = pltpu.make_async_copy(a_in.at[:, columns(r)], a_full.at[pl.ds(r * depth, depth), :], local_sem.at[0])
    own_a.start()
    own_w = pltpu.make_async_copy(w_in.at[:, columns(r)], w_full.at[pl.ds(r * rows, rows), :], local_sem.at[2])
    own_w.start()
    ranks = b_in.shape[1]
    lane = lax.broadcasted_iota(jnp.int32, (1, ranks), 1)
    weights = jnp.zeros((1, ranks), jnp.float32)
    for k in range(ranks // RANK):
        here = (lane >= k * RANK) & (lane < (k + 1) * RANK)
        weights = jnp.where(here, s_in[c * (ranks // RANK) + k], weights)
    load.wait()

    @pl.loop(0, rows // QB)
    def _(y):
        from_row = pl.multiple_of(y * QB, QB)
        b_full[c, pl.ds(pl.multiple_of(r * rows + y * QB, QB), QB), :] = (
            b_raw[pl.ds(from_row, QB), :].astype(jnp.float32) * weights).astype(jnp.bfloat16)

    b_plane(r, gate).start()
    for m in range(1, half):
        b_plane(r, mate(m)).start()

    for i in range(1, nr):
        pltpu.make_async_remote_copy(
            src_ref=a_in.at[:, columns(z_peer(i))], dst_ref=a_full.at[pl.ds(r * depth, depth), :],
            send_sem=a_send.at[i], recv_sem=a_recv.at[r],
            device_id={"row": z_peer(i)}, device_id_type=pl.DeviceIdType.MESH).start()
    def w_copy(i, t):
        source = pl.multiple_of(t * CHUNK, CHUNK)
        return pltpu.make_async_remote_copy(
            src_ref=w_in.at[pl.ds(source, CHUNK), columns(z_peer(i))],
            dst_ref=w_full.at[pl.ds(pl.multiple_of(r * rows + t * CHUNK, CHUNK), CHUNK), :],
            send_sem=w_send.at[i, t], recv_sem=w_recv.at[r, t],
            device_id={"row": z_peer(i)}, device_id_type=pl.DeviceIdType.MESH)

    def b_wait(j, q):
        slot = b_slot(j, q)
        pltpu.make_async_copy(slot, slot, b_recv.at[j, q]).wait()

    def b_share(k, j, q, to, src):
        return pltpu.make_async_remote_copy(
            src_ref=src, dst_ref=b_slot(j, q), send_sem=b_send.at[k[0], k[1]], recv_sem=b_recv.at[j, q],
            device_id={"col": to}, device_id_type=pl.DeviceIdType.MESH)

    for i in range(1, nr):
        w_copy(i, 0).start()

    def spread(j):
        for i in range(1, planes):
            b_share((j, i), j, c, plane_peer(i), b_slot(j, c)).start()
        b_share((j, planes), j, c, sibling, b_slot(j, c)).start()

    spread(r)
    for m in range(1, half):
        b_wait(mate(m), c)
        spread(mate(m))
    for m in range(half):
        j = half - own_half + m
        b_wait(j, c)

        @pl.when(r == inner)
        def _(j=j):
            for k in range(1, half):
                b_plane(j, mate(k)).start()

        spread(j)

    @pl.loop(0, nr)
    def _(j):
        for i in range(1, planes):
            q = plane_peer(i)
            b_wait(j, q)
            b_share((j, planes + i), j, q, sibling, b_slot(j, q)).start()

    @pl.loop(1, chunks)
    def _(t):
        for i in range(1, nr):
            w_copy(i, t).start()

    @pl.loop(0, nr)
    def _(j):
        for i in range(planes):
            b_wait(j, lax.rem(chip + i, planes) * 2 + (1 - core))

    own_a.wait()
    for i in range(1, nr):
        part = a_full.at[pl.ds(z_peer(i) * depth, depth), :]
        pltpu.make_async_copy(part, part, a_recv.at[z_peer(i)]).wait()

    def merge_cols(j, t, col, count):
        row = pl.multiple_of(j * rows + t * CHUNK, CHUNK)
        at = pl.ds(row, CHUNK)
        lhs = jnp.concatenate([b_full[q, at, :] for q in range(nc)], axis=1)
        part = pl.ds(pl.multiple_of(col * QB, QB), count * QB)
        merged = w_full[at, part].astype(jnp.float32) + jnp.dot(
            lhs, a_full[:, part], preferred_element_type=jnp.float32)
        for y in range(per_chunk):
            for x in range(count):
                tile = merged[y * QB:(y + 1) * QB, x * QB:(x + 1) * QB]
                largest = jnp.max(jnp.max(jnp.abs(tile), axis=0, keepdims=True), axis=1, keepdims=True) + 1e-06
                w_full[pl.ds(pl.multiple_of(row + y * QB, QB), QB), pl.ds(pl.multiple_of((col + x) * QB, QB), QB)] = (
                    tile / largest).astype(jnp.bfloat16)
                s_own[j, t * per_chunk + y, pl.ds(col + x, 1), :] = jnp.broadcast_to(largest, (1, QB))

    def merge_chunk(j, t):
        @pl.loop(0, blocks // 2)
        def _(pair):
            merge_cols(j, t, pair * 2, 2)

        if blocks % 2:
            merge_cols(j, t, blocks - 1, 1)

    own_w.wait()

    @pl.loop(0, chunks)
    def _(t):
        merge_chunk(r, t)

    @pl.loop(0, chunks * (nr - 1))
    def _(n):
        t = n // (nr - 1)
        j = lax.rem(r + 1 + lax.rem(n, nr - 1), nr)
        part = w_full.at[pl.ds(pl.multiple_of(j * rows + t * CHUNK, CHUNK), CHUNK), :]
        pltpu.make_async_copy(part, part, w_recv.at[j, t]).wait()
        merge_chunk(j, t)

    def s_copy(i):
        return pltpu.make_async_remote_copy(
            src_ref=s_own.at[z_peer(i)], dst_ref=s_all.at[r], send_sem=s_send.at[i], recv_sem=s_recv.at[r],
            device_id={"row": z_peer(i)}, device_id_type=pl.DeviceIdType.MESH)

    for i in range(1, nr):
        s_copy(i).start()
    s_all[r] = s_own[r]
    for i in range(1, nr):
        pltpu.make_async_copy(s_own.at[0], s_all.at[z_peer(i)], s_recv.at[z_peer(i)]).wait()
    to_out = pltpu.make_async_copy(s_all, scales_out, local_sem.at[3])
    to_out.start()

    for i in range(1, nr):
        s_copy(i).wait_send()
        part = a_full.at[pl.ds(r * depth, depth), :]
        pltpu.make_async_copy(part, part, a_send.at[i]).wait()

    @pl.loop(0, nr)
    def _(j):
        for k in range(1, 2 * planes):
            pltpu.make_async_copy(b_in, b_in, b_send.at[j, k]).wait()

    b_plane(r, gate).wait_send()
    for m in range(1, half):
        b_plane(r, mate(m)).wait_send()

    @pl.when(r == inner)
    def _():
        for m in range(half):
            for k in range(1, half):
                b_plane(half - own_half + m, mate(k)).wait_send()

    @pl.loop(0, chunks)
    def _(t):
        for i in range(1, nr):
            w_copy(i, t).wait_send()

    to_out.wait()


def merge(nr, nc, adapter_weights, b, a, w):
    rows, width = w.shape
    cols = width // nr
    depth = a.shape[0]
    chunks = rows // CHUNK
    blocks = cols // QB
    dma = pltpu.SemaphoreType.DMA
    return pl.pallas_call(
        functools.partial(merge_kernel, nr, nc),
        out_shape=[
            jax.ShapeDtypeStruct((nr * rows, cols), jnp.bfloat16),
            jax.ShapeDtypeStruct((nr, rows // QB, blocks, QB), jnp.float32),
        ],
        in_specs=[pl.BlockSpec(memory_space=pltpu.SMEM)] + [pl.BlockSpec(memory_space=pltpu.HBM)] * 3,
        out_specs=[pl.BlockSpec(memory_space=pltpu.VMEM), pl.BlockSpec(memory_space=pltpu.HBM)],
        scratch_shapes=[
            pltpu.VMEM((nr * depth, cols), jnp.bfloat16),
            pltpu.VMEM(b.shape, jnp.bfloat16),
            pltpu.VMEM((nc, nr * rows, b.shape[1]), jnp.bfloat16),
            pltpu.VMEM((nr, rows // QB, blocks, QB), jnp.float32),
            pltpu.VMEM((nr, rows // QB, blocks, QB), jnp.float32),
            dma((nr,)), dma((nr,)),
            dma((nr, nc)), dma((nr, nc)), dma((nr, nr)),
            dma((nr, chunks)), dma((nr, chunks)),
            dma((nr,)), dma((nr,)),
            dma((4,)),
        ],
        compiler_params=pltpu.CompilerParams(
            collective_id=0, has_side_effects=True, vmem_limit_bytes=32 * 2 ** 20),
        cost_estimate=pl.CostEstimate(
            flops=2 * nr * rows * nr * depth * cols, bytes_accessed=4 * rows * width, transcendentals=0),
    )(adapter_weights, b, a, w)


def store_kernel(parts, values, out, sem):
    count = values.shape[0] // parts
    copies = [
        pltpu.make_async_copy(values.at[pl.ds(i * count, count), :], out.at[pl.ds(i * count, count), :], sem.at[i])
        for i in range(parts)
    ]
    for copy in copies:
        copy.start()
    for copy in copies:
        copy.wait()


def store(values, parts):
    return pl.pallas_call(
        functools.partial(store_kernel, parts),
        out_shape=jax.ShapeDtypeStruct(values.shape, values.dtype),
        in_specs=[pl.BlockSpec(memory_space=pltpu.VMEM)],
        out_specs=pl.BlockSpec(memory_space=pltpu.HBM),
        scratch_shapes=[pltpu.SemaphoreType.DMA((parts,))],
        compiler_params=pltpu.CompilerParams(vmem_limit_bytes=2 ** 20),
    )(values)


def serving_shards(nr, nc, pretrained_weight, up_factors, down_factors, adapter_weights):
    values, scales = merge(nr, nc, adapter_weights, up_factors, down_factors, pretrained_weight)
    largest = jnp.transpose(scales[:, :, :, 0], (1, 0, 2)).reshape(scales.shape[1], -1)
    return (store(values, 8), largest)


def solution(mesh):
    nr, nc = mesh.shape["row"], mesh.shape["col"]

    def shards(pretrained_weight, up_factors, down_factors, adapter_weights):
        rows, width = pretrained_weight.shape
        whole_blocks = width % (nr * QB) == 0 and rows % CHUNK == 0 and nc % 2 == 0 and nr % 2 == 0
        if whole_blocks and up_factors.shape[1] % QB == 0:
            return serving_shards(nr, nc, pretrained_weight, up_factors, down_factors, adapter_weights)
        return panel_shards(pretrained_weight, up_factors, down_factors, adapter_weights)

    return jax.shard_map(
        shards,
        mesh=mesh,
        in_specs=(P("row", "col"), P("row", "col"), P("row", "col"), P()),
        out_specs=(P(None, ("col", "row")), P("row", "col")),
        check_vma=False,
    )
```

```python
import functools

import jax
import jax.numpy as jnp
from jax import lax
from jax.experimental import pallas as pl
from jax.experimental.pallas import tpu as pltpu
from jax.sharding import PartitionSpec as P

RANK = 64
QB = 128
CHUNK = 128


def weighted_factors(up_factors, adapter_weights):
    local_rank_slab = up_factors.shape[1]
    broadcast_scales = jnp.repeat(adapter_weights, RANK)
    offset = lax.axis_index("col") * local_rank_slab
    local_scale = lax.dynamic_slice_in_dim(broadcast_scales, offset, local_rank_slab, 0)
    return (up_factors.astype(jnp.float32) * local_scale[None, :]).astype(jnp.bfloat16)


def scale_tiles(merged_weight):
    row_count, col_count = merged_weight.shape
    tiles = merged_weight.reshape(row_count // QB, QB, col_count // QB, QB)
    largest = jnp.max(jnp.abs(tiles), axis=(1, 3)) + 1e-06
    values = (tiles / largest[:, None, :, None]).astype(jnp.bfloat16).reshape(row_count, col_count)
    return (values, largest)


def panel_shards(pretrained_weight, up_factors, down_factors, adapter_weights):
    weighted_update = weighted_factors(up_factors, adapter_weights)
    b_panel = lax.all_gather(weighted_update, "col", axis=1, tiled=True)
    merged_weight = pretrained_weight.astype(jnp.float32) + jnp.dot(
        b_panel,
        lax.all_gather(down_factors, "row", axis=0, tiled=True),
        preferred_element_type=jnp.float32,
    )
    values, largest = scale_tiles(merged_weight)
    serving = lax.all_to_all(values, "row", split_axis=1, concat_axis=0, tiled=True)
    return (serving, largest)


def merge_kernel(
    nr, nc, s_in, b_in, a_in, w_in, w_full, scales_out,
    a_full, b_raw, b_full, s_own, s_all,
    a_send, a_recv, b_send, b_recv, line_send, w_send, w_recv, s_send, s_recv, local_sem,
):
    rows, width = w_in.shape
    cols = width // nr
    depth = a_in.shape[0]
    planes = nc // 2
    chunks = rows // CHUNK
    per_chunk = CHUNK // QB
    blocks = cols // QB
    r = lax.axis_index("row")
    c = lax.axis_index("col")
    chip, core = c // 2, lax.rem(c, 2)
    sibling = chip * 2 + (1 - core)

    def z_peer(i):
        return lax.rem(r + i, nr)

    def plane_peer(i):
        return lax.rem(chip + i, planes) * 2 + core

    barrier = pltpu.get_barrier_semaphore()
    for i in range(1, nr):
        pl.semaphore_signal(barrier, inc=1, device_id={"row": z_peer(i)}, device_id_type=pl.DeviceIdType.MESH)
    for i in range(1, planes):
        pl.semaphore_signal(barrier, inc=1, device_id={"col": plane_peer(i)}, device_id_type=pl.DeviceIdType.MESH)
    pl.semaphore_signal(barrier, inc=1, device_id={"col": sibling}, device_id_type=pl.DeviceIdType.MESH)
    pl.semaphore_wait(barrier, nr - 1 + planes - 1 + 1)

    def columns(j):
        return pl.ds(pl.multiple_of(j * cols, QB), cols)

    def b_slot(j, q):
        return b_full.at[q, pl.ds(j * rows, rows), :]

    half = nr // 2
    own_half = r // half * half
    gate = jnp.where(own_half == 0, half, half - 1)
    inner = jnp.where(own_half == 0, half - 1, half)

    def mate(m):
        return own_half + lax.rem(r - own_half + m, half)

    def b_plane(j, to):
        return pltpu.make_async_remote_copy(
            src_ref=b_slot(j, c), dst_ref=b_slot(j, c), send_sem=line_send.at[j, to], recv_sem=b_recv.at[j, c],
            device_id={"row": to}, device_id_type=pl.DeviceIdType.MESH)

    load = pltpu.make_async_copy(b_in, b_raw, local_sem.at[1])
    load.start()
    own_a = pltpu.make_async_copy(a_in.at[:, columns(r)], a_full.at[pl.ds(r * depth, depth), :], local_sem.at[0])
    own_a.start()
    own_w = pltpu.make_async_copy(w_in.at[:, columns(r)], w_full.at[pl.ds(r * rows, rows), :], local_sem.at[2])
    own_w.start()
    ranks = b_in.shape[1]
    lane = lax.broadcasted_iota(jnp.int32, (1, ranks), 1)
    weights = jnp.zeros((1, ranks), jnp.float32)
    for k in range(ranks // RANK):
        here = (lane >= k * RANK) & (lane < (k + 1) * RANK)
        weights = jnp.where(here, s_in[c * (ranks // RANK) + k], weights)
    load.wait()

    @pl.loop(0, rows // QB)
    def _(y):
        from_row = pl.multiple_of(y * QB, QB)
        b_full[c, pl.ds(pl.multiple_of(r * rows + y * QB, QB), QB), :] = (
            b_raw[pl.ds(from_row, QB), :].astype(jnp.float32) * weights).astype(jnp.bfloat16)

    b_plane(r, gate).start()
    for m in range(1, half):
        b_plane(r, mate(m)).start()

    for i in range(1, nr):
        pltpu.make_async_remote_copy(
            src_ref=a_in.at[:, columns(z_peer(i))], dst_ref=a_full.at[pl.ds(r * depth, depth), :],
            send_sem=a_send.at[i], recv_sem=a_recv.at[r],
            device_id={"row": z_peer(i)}, device_id_type=pl.DeviceIdType.MESH).start()
    def w_copy(i, t):
        source = pl.multiple_of(t * CHUNK, CHUNK)
        return pltpu.make_async_remote_copy(
            src_ref=w_in.at[pl.ds(source, CHUNK), columns(z_peer(i))],
            dst_ref=w_full.at[pl.ds(pl.multiple_of(r * rows + t * CHUNK, CHUNK), CHUNK), :],
            send_sem=w_send.at[i, t], recv_sem=w_recv.at[r, t],
            device_id={"row": z_peer(i)}, device_id_type=pl.DeviceIdType.MESH)

    def b_wait(j, q):
        slot = b_slot(j, q)
        pltpu.make_async_copy(slot, slot, b_recv.at[j, q]).wait()

    def b_share(k, j, q, to, src):
        return pltpu.make_async_remote_copy(
            src_ref=src, dst_ref=b_slot(j, q), send_sem=b_send.at[k[0], k[1]], recv_sem=b_recv.at[j, q],
            device_id={"col": to}, device_id_type=pl.DeviceIdType.MESH)

    for i in range(1, nr):
        w_copy(i, 0).start()

    def spread(j):
        for i in range(1, planes):
            b_share((j, i), j, c, plane_peer(i), b_slot(j, c)).start()
        b_share((j, planes), j, c, sibling, b_slot(j, c)).start()

    spread(r)
    for m in range(1, half):
        b_wait(mate(m), c)
        spread(mate(m))
    for m in range(half):
        j = half - own_half + m
        b_wait(j, c)

        @pl.when(r == inner)
        def _(j=j):
            for k in range(1, half):
                b_plane(j, mate(k)).start()

        spread(j)

    @pl.loop(0, nr)
    def _(j):
        for i in range(1, planes):
            q = plane_peer(i)
            b_wait(j, q)
            b_share((j, planes + i), j, q, sibling, b_slot(j, q)).start()

    @pl.loop(1, chunks)
    def _(t):
        for i in range(1, nr):
            w_copy(i, t).start()

    @pl.loop(0, nr)
    def _(j):
        for i in range(planes):
            b_wait(j, lax.rem(chip + i, planes) * 2 + (1 - core))

    own_a.wait()
    for i in range(1, nr):
        part = a_full.at[pl.ds(z_peer(i) * depth, depth), :]
        pltpu.make_async_copy(part, part, a_recv.at[z_peer(i)]).wait()

    def merge_cols(j, t, col, count):
        row = pl.multiple_of(j * rows + t * CHUNK, CHUNK)
        at = pl.ds(row, CHUNK)
        lhs = jnp.concatenate([b_full[q, at, :] for q in range(nc)], axis=1)
        part = pl.ds(pl.multiple_of(col * QB, QB), count * QB)
        merged = w_full[at, part].astype(jnp.float32) + jnp.dot(
            lhs, a_full[:, part], preferred_element_type=jnp.float32)
        for y in range(per_chunk):
            for x in range(count):
                tile = merged[y * QB:(y + 1) * QB, x * QB:(x + 1) * QB]
                largest = jnp.max(jnp.max(jnp.abs(tile), axis=0, keepdims=True), axis=1, keepdims=True) + 1e-06
                w_full[pl.ds(pl.multiple_of(row + y * QB, QB), QB), pl.ds(pl.multiple_of((col + x) * QB, QB), QB)] = (
                    tile / largest).astype(jnp.bfloat16)
                s_own[j, t * per_chunk + y, pl.ds(col + x, 1), :] = jnp.broadcast_to(largest, (1, QB))

    def merge_chunk(j, t):
        @pl.loop(0, blocks // 2)
        def _(pair):
            merge_cols(j, t, pair * 2, 2)

        if blocks % 2:
            merge_cols(j, t, blocks - 1, 1)

    own_w.wait()

    @pl.loop(0, chunks)
    def _(t):
        merge_chunk(r, t)

    @pl.loop(0, chunks * (nr - 1))
    def _(n):
        t = n // (nr - 1)
        j = lax.rem(r + 1 + lax.rem(n, nr - 1), nr)
        part = w_full.at[pl.ds(pl.multiple_of(j * rows + t * CHUNK, CHUNK), CHUNK), :]
        pltpu.make_async_copy(part, part, w_recv.at[j, t]).wait()
        merge_chunk(j, t)

    def s_copy(i):
        return pltpu.make_async_remote_copy(
            src_ref=s_own.at[z_peer(i)], dst_ref=s_all.at[r], send_sem=s_send.at[i], recv_sem=s_recv.at[r],
            device_id={"row": z_peer(i)}, device_id_type=pl.DeviceIdType.MESH)

    for i in range(1, nr):
        s_copy(i).start()
    s_all[r] = s_own[r]
    for i in range(1, nr):
        pltpu.make_async_copy(s_own.at[0], s_all.at[z_peer(i)], s_recv.at[z_peer(i)]).wait()
    to_out = pltpu.make_async_copy(s_all, scales_out, local_sem.at[3])
    to_out.start()

    for i in range(1, nr):
        s_copy(i).wait_send()
        part = a_full.at[pl.ds(r * depth, depth), :]
        pltpu.make_async_copy(part, part, a_send.at[i]).wait()

    @pl.loop(0, nr)
    def _(j):
        for k in range(1, 2 * planes):
            pltpu.make_async_copy(b_in, b_in, b_send.at[j, k]).wait()

    b_plane(r, gate).wait_send()
    for m in range(1, half):
        b_plane(r, mate(m)).wait_send()

    @pl.when(r == inner)
    def _():
        for m in range(half):
            for k in range(1, half):
                b_plane(half - own_half + m, mate(k)).wait_send()

    @pl.loop(0, chunks)
    def _(t):
        for i in range(1, nr):
            w_copy(i, t).wait_send()

    to_out.wait()


def merge(nr, nc, adapter_weights, b, a, w):
    rows, width = w.shape
    cols = width // nr
    depth = a.shape[0]
    chunks = rows // CHUNK
    blocks = cols // QB
    dma = pltpu.SemaphoreType.DMA
    return pl.pallas_call(
        functools.partial(merge_kernel, nr, nc),
        out_shape=[
            jax.ShapeDtypeStruct((nr * rows, cols), jnp.bfloat16),
            jax.ShapeDtypeStruct((nr, rows // QB, blocks, QB), jnp.float32),
        ],
        in_specs=[pl.BlockSpec(memory_space=pltpu.SMEM)] + [pl.BlockSpec(memory_space=pltpu.HBM)] * 3,
        out_specs=[pl.BlockSpec(memory_space=pltpu.VMEM), pl.BlockSpec(memory_space=pltpu.HBM)],
        scratch_shapes=[
            pltpu.VMEM((nr * depth, cols), jnp.bfloat16),
            pltpu.VMEM(b.shape, jnp.bfloat16),
            pltpu.VMEM((nc, nr * rows, b.shape[1]), jnp.bfloat16),
            pltpu.VMEM((nr, rows // QB, blocks, QB), jnp.float32),
            pltpu.VMEM((nr, rows // QB, blocks, QB), jnp.float32),
            dma((nr,)), dma((nr,)),
            dma((nr, nc)), dma((nr, nc)), dma((nr, nr)),
            dma((nr, chunks)), dma((nr, chunks)),
            dma((nr,)), dma((nr,)),
            dma((4,)),
        ],
        compiler_params=pltpu.CompilerParams(
            collective_id=0, has_side_effects=True, vmem_limit_bytes=32 * 2 ** 20),
        cost_estimate=pl.CostEstimate(
            flops=2 * nr * rows * nr * depth * cols, bytes_accessed=4 * rows * width, transcendentals=0),
    )(adapter_weights, b, a, w)


def store_kernel(parts, values, out, sem):
    count = values.shape[0] // parts
    copies = [
        pltpu.make_async_copy(values.at[pl.ds(i * count, count), :], out.at[pl.ds(i * count, count), :], sem.at[i])
        for i in range(parts)
    ]
    for copy in copies:
        copy.start()
    for copy in copies:
        copy.wait()


def store(values, parts):
    return pl.pallas_call(
        functools.partial(store_kernel, parts),
        out_shape=jax.ShapeDtypeStruct(values.shape, values.dtype),
        in_specs=[pl.BlockSpec(memory_space=pltpu.VMEM)],
        out_specs=pl.BlockSpec(memory_space=pltpu.HBM),
        scratch_shapes=[pltpu.SemaphoreType.DMA((parts,))],
        compiler_params=pltpu.CompilerParams(vmem_limit_bytes=2 ** 20),
    )(values)


def serving_shards(nr, nc, pretrained_weight, up_factors, down_factors, adapter_weights):
    values, scales = merge(nr, nc, adapter_weights, up_factors, down_factors, pretrained_weight)
    largest = jnp.transpose(scales[:, :, :, 0], (1, 0, 2)).reshape(scales.shape[1], -1)
    return (store(values, 8), largest)


def solution(mesh):
    nr, nc = mesh.shape["row"], mesh.shape["col"]

    def shards(pretrained_weight, up_factors, down_factors, adapter_weights):
        rows, width = pretrained_weight.shape
        whole_blocks = width % (nr * QB) == 0 and rows % CHUNK == 0 and nc % 2 == 0 and nr % 2 == 0
        if whole_blocks and up_factors.shape[1] % QB == 0:
            return serving_shards(nr, nc, pretrained_weight, up_factors, down_factors, adapter_weights)
        return panel_shards(pretrained_weight, up_factors, down_factors, adapter_weights)

    return jax.shard_map(
        shards,
        mesh=mesh,
        in_specs=(P("row", "col"), P("row", "col"), P("row", "col"), P()),
        out_specs=(P(None, ("col", "row")), P("row", "col")),
        check_vma=False,
    )
```
